32 devices in a mesh: groups: 2 (over x), expert: 16 (over z, y, core).
Axes of the slice: x: 2, y: 2, z: 4, core: 2. Of those that a mesh axis runs over, the one named last changes fastest.
Arguments:
- tokens: bfloat16 [2, 2048, 2048], P(None, ('groups', 'expert')), parts along dimension 1, may hold values from -6 to 6
- route_ids: int32 [2, 2048, 2], P(None, ('groups', 'expert')), parts along dimension 1, may hold values from 0 to 15, as said below
- route_slots: int32 [2, 2048, 2], P(None, ('groups', 'expert')), parts along dimension 1, may hold values from 0 to 15, as said below
- mod_shift: float32 [4, 2048], P('groups'), parts along dimension 0, may hold values from -4 to 4
- mod_scale: float32 [4, 2048], P('groups'), parts along dimension 0, may hold values from -4 to 4
- mod_gate: float32 [4, 2048], P('groups'), parts along dimension 0, may hold values from 0.1 to 1.9
- guidance: float32 [2], P('groups'), parts along dimension 0, may hold values from 2 to 6
- router_weight: bfloat16 [2048, 16], replicated, may hold values from -0.125 to 0.125
- expert_gate: bfloat16 [16, 2048, 768], P('expert'), may hold values from -0.125 to 0.125
- expert_up: bfloat16 [16, 2048, 768], P('expert'), may hold values from -0.125 to 0.125
- expert_down: bfloat16 [16, 768, 2048], P('expert'), may hold values from -0.21875 to 0.21875
- shared_gate: bfloat16 [2048, 1408], P('expert'), may hold values from -0.125 to 0.125
- shared_up: bfloat16 [2048, 1408], P('expert'), may hold values from -0.125 to 0.125
- shared_down: bfloat16 [1408, 2048], P(None, 'expert'), may hold values from -0.15625 to 0.15625
- head_weight: bfloat16 [2048, 128], replicated, may hold values from -0.125 to 0.125
Outputs:
- hidden_out: bfloat16 [2, 2048, 2048], P(None, ('groups', 'expert')), parts along dimension 1
- guided: float32 [2048, 128], P(('groups', 'expert')), parts along dimension 0
The draws below stay inside these ranges and needn't reach their ends.
There are 2 independent parts, one for each index of `groups`. The reference program is written for one: setup_inputs(seed, part) draws one part's arguments, and reference() takes and returns one part's arrays. A program takes and returns all parts, laid end to end along the dimension named above; an argument that names none is the same for every part. Nothing has to cross between parts.
Inputs may be any that keep to these rules, and one draw needn't show every extreme that they name: `route_ids`: for each half, the 64 tokens of one device name each expert at most 16 times in all; this is met by some expert on every device, and one expert is named 16 times by every device's tokens of both halves. A token's 2 experts differ. `route_slots`: within one half and one device, the choices that name one expert hold the distinct rows 0 to their number minus 1, in the same place as the expert in route_ids.
All inputs are finite; a program needn't handle non-finite values.
Results may differ from the reference program's by a relative error of at most 0.0067.
Values may be sent and summed in bfloat16 or wider, within the bound.
A program may use at most 128 MiB of HBM per device.

```python
import jax
import jax.numpy as jnp
from jax import lax

D = 2048
FFE = 768
FS = 1408
TOPK = 2
OUTC = 128
HALF_DEV = 64
EXPERTS = 16
CAP = 16
TOKENS_HALF = 1024
N_EXPERT = 16


def block_routes(block_key, hot_global):
    cost_key, hot_key, order_key = jax.random.split(block_key, 3)
    expert_index = jnp.arange(EXPERTS, dtype=jnp.int32)
    costs = jax.random.randint(cost_key, (EXPERTS,), 3, 10, dtype=jnp.int32)
    hot_local = jax.random.randint(hot_key, (), 0, EXPERTS, dtype=jnp.int32)
    costs = jnp.where((expert_index == hot_global) | (expert_index == hot_local), 1, costs)
    slot_index = jnp.arange(CAP, dtype=jnp.int32)
    ranking = (slot_index[None, :] + 1) * costs[:, None] * EXPERTS + expert_index[:, None]
    ranking = ranking.reshape(-1)
    assigned = TOPK * HALF_DEV
    ranks = jnp.argsort(jnp.argsort(ranking))
    taken = ranks < assigned
    pool = jnp.arange(EXPERTS * CAP, dtype=jnp.int32)
    listed = jnp.sort(jnp.where(taken, pool, EXPERTS * CAP))[:assigned]
    experts_listed = (listed // CAP).reshape(TOPK, HALF_DEV).T
    slots_listed = (listed % CAP).reshape(TOPK, HALF_DEV).T
    shuffle = jax.random.permutation(order_key, HALF_DEV)
    return (experts_listed[shuffle].astype(jnp.int32), slots_listed[shuffle].astype(jnp.int32))


def routing_tables(key):
    base_key = jax.random.fold_in(key, 9103)
    hot_global = jax.random.randint(jax.random.fold_in(base_key, 1), (), 0, EXPERTS, dtype=jnp.int32)
    block_keys = jax.random.split(jax.random.fold_in(base_key, 2), 2 * N_EXPERT)
    chosen_ids, chosen_slots = jax.vmap(block_routes, in_axes=(0, None))(block_keys, hot_global)
    chosen_ids = chosen_ids.reshape(2, N_EXPERT * HALF_DEV, TOPK)
    chosen_slots = chosen_slots.reshape(2, N_EXPERT * HALF_DEV, TOPK)
    return (chosen_ids, chosen_slots)


def draw_route_ids(key, part):
    return routing_tables(key)[0]


def draw_route_slots(key, part):
    return routing_tables(key)[1]


def shard_levels(own_key, shape, cuts, smallest, high):
    def one(axis_at, parts):
        steps = jax.random.uniform(jax.random.fold_in(jax.random.fold_in(own_key, 6), axis_at), (parts,), jnp.float32, smallest / len(cuts), high / len(cuts))
        return jnp.repeat(jnp.exp(steps), shape[axis_at] // parts).reshape((-1,) + (1,) * (len(shape) - axis_at - 1))

    factor_of = one(*cuts[0])
    for cut in cuts[1:]:
        factor_of = factor_of * one(*cut)
    return factor_of


def bell_draw(rng, dims, deviation, limit, pieces=(), kind=jnp.bfloat16):
    entries = jax.random.normal(rng, dims, jnp.float32) * deviation
    if len(pieces) > 0:
        entries = shard_levels(rng, dims, pieces, -0.22, 0.18) * entries
    return jnp.clip(entries, min=-limit, max=limit).astype(kind)


def setup_inputs(seed: int = 0, part: int = 0) -> dict:
    key_of = jax.random.split(jax.random.key(seed), 16)
    part_splits = jax.random.split(jax.random.fold_in(key_of[15], part), 16)
    tokens = bell_draw(part_splits[0], (2, TOKENS_HALF, D), 1.0, 6.0, ((1, 16),))
    route_ids = draw_route_ids(jax.random.fold_in(jax.random.fold_in(key_of[15], part), 71), part)
    route_slots = draw_route_slots(jax.random.fold_in(jax.random.fold_in(key_of[15], part), 71), part)
    mod_shift = bell_draw(part_splits[3], (2, D), 0.5, 4.0, (), jnp.float32)
    mod_scale = bell_draw(part_splits[4], (2, D), 0.5, 4.0, (), jnp.float32)
    mod_gate = jnp.clip(1.0 + 0.18 * jax.random.normal(part_splits[5], (2, D), jnp.float32), 0.1, 1.9)
    guidance = jnp.clip(jax.random.uniform(part_splits[6], (1,), jnp.float32, 2.0, 6.0), 2.0, 6.0)
    router_weight = bell_draw(key_of[7], (D, EXPERTS), D ** -0.5, 0.125)
    expert_gate = bell_draw(key_of[8], (EXPERTS, D, FFE), D ** -0.5, 0.125, ((0, 16),))
    expert_up = bell_draw(key_of[9], (EXPERTS, D, FFE), D ** -0.5, 0.125, ((0, 16),))
    expert_down = bell_draw(key_of[10], (EXPERTS, FFE, D), FFE ** -0.5, 0.21875, ((0, 16),))
    shared_gate = bell_draw(key_of[11], (D, FS), D ** -0.5, 0.125, ((0, 16),))
    shared_up = bell_draw(key_of[12], (D, FS), D ** -0.5, 0.125, ((0, 16),))
    shared_down = bell_draw(key_of[13], (FS, D), FS ** -0.5, 0.15625, ((1, 16),))
    head_weight = bell_draw(key_of[14], (D, OUTC), D ** -0.5, 0.125)
    return dict(tokens=tokens, route_ids=route_ids, route_slots=route_slots, mod_shift=mod_shift, mod_scale=mod_scale, mod_gate=mod_gate, guidance=guidance, router_weight=router_weight, expert_gate=expert_gate, expert_up=expert_up, expert_down=expert_down, shared_gate=shared_gate, shared_up=shared_up, shared_down=shared_down, head_weight=head_weight)


epsilon = 1e-06

def layer_norm(values):
    center = values - lax.optimization_barrier(jnp.mean(values, axis=-1, keepdims=True))
    spread = lax.optimization_barrier(jnp.mean(center * center, axis=-1, keepdims=True))
    return center * lax.rsqrt(spread + epsilon)

def swiglu_rows(row_block, w_gate, w_up, w_down):
    gate_part = jnp.dot(row_block, w_gate, preferred_element_type=jnp.float32)
    up_part = jnp.dot(row_block, w_up, preferred_element_type=jnp.float32)
    hidden = (jax.nn.silu(gate_part) * up_part).astype(jnp.bfloat16)
    return jnp.dot(hidden, w_down, preferred_element_type=jnp.float32)

def one_expert(operands):
    row_block, w_gate, w_up, w_down = operands
    return swiglu_rows(row_block, w_gate, w_up, w_down).astype(jnp.bfloat16)

def reference(tokens, route_ids, route_slots, mod_shift, mod_scale, mod_gate, guidance, router_weight, expert_gate, expert_up, expert_down, shared_gate, shared_up, shared_down, head_weight):
    model_width = tokens.shape[-1]
    inputs = tokens.astype(jnp.float32)
    modulated = (layer_norm(inputs) * (1.0 + mod_scale[:, None, :]) + mod_shift[:, None, :]).astype(jnp.bfloat16)
    flat_rows = modulated.reshape(2 * TOKENS_HALF, model_width)
    logits = jnp.dot(flat_rows, router_weight, preferred_element_type=jnp.float32).reshape(2, TOKENS_HALF, EXPERTS)
    picked = jnp.take_along_axis(logits, route_ids, axis=2)
    affinity = jax.nn.sigmoid(picked)
    weights = affinity / lax.optimization_barrier(jnp.sum(affinity, axis=2, keepdims=True))
    device_of = jnp.arange(TOKENS_HALF, dtype=jnp.int32) // HALF_DEV
    halves = jnp.arange(2, dtype=jnp.int32)
    position = ((halves[:, None, None] * N_EXPERT + device_of[None, :, None]) * EXPERTS + route_ids) * CAP + route_slots
    position = position.reshape(-1).astype(jnp.int32)
    total_rows = 2 * N_EXPERT * EXPERTS * CAP
    sources = jnp.broadcast_to(modulated[:, :, None, :], (2, TOKENS_HALF, TOPK, model_width)).reshape(-1, model_width)
    buffer = jnp.zeros((total_rows, model_width), jnp.bfloat16).at[position].set(sources)
    by_expert = buffer.reshape(2 * N_EXPERT, EXPERTS, CAP, model_width).transpose(1, 0, 2, 3)
    by_expert = by_expert.reshape(EXPERTS, 2 * N_EXPERT * CAP, model_width)
    outputs = lax.map(one_expert, (by_expert, expert_gate, expert_up, expert_down))
    returned = outputs.reshape(EXPERTS, 2 * N_EXPERT, CAP, model_width).transpose(1, 0, 2, 3).reshape(total_rows, model_width)
    chosen = returned[position].reshape(2, TOKENS_HALF, TOPK, model_width).astype(jnp.float32)
    routed = lax.optimization_barrier(jnp.sum(weights[..., None] * chosen, axis=2))
    shared = swiglu_rows(flat_rows, shared_gate, shared_up, shared_down).reshape(2, TOKENS_HALF, model_width)
    hidden_out = (inputs + mod_gate[:, None, :] * (routed + shared)).astype(jnp.bfloat16)
    final_norm = layer_norm(hidden_out.astype(jnp.float32)).astype(jnp.bfloat16)
    predicted = jnp.dot(final_norm.reshape(2 * TOKENS_HALF, model_width), head_weight, preferred_element_type=jnp.float32)
    predicted = predicted.reshape(2, TOKENS_HALF, OUTC)
    guided = predicted[1] + guidance[0] * (predicted[0] - predicted[1])
    return (hidden_out, guided)
```

```python
import functools
import math

import jax
import jax.numpy as jnp
from jax import lax
from jax.experimental import pallas as pl
from jax.experimental.pallas import tpu as pltpu
from jax.sharding import PartitionSpec as P

epsilon = 1e-06
MESH = pl.DeviceIdType.MESH


def layer_norm(values):
    center = values - jnp.mean(values, axis=-1, keepdims=True)
    spread = jnp.mean(center * center, axis=-1, keepdims=True)
    return center * lax.rsqrt(spread + epsilon)


def expert_block(received, w_gate, w_up, w_down):
    array_shape = received.shape
    local_count = w_gate.shape[0]
    middle = math.prod(array_shape[1:-1])
    row_block = received.reshape(
        array_shape[0] // local_count, local_count, middle, array_shape[-1]
    )
    gate_part = jnp.einsum("semd,edf->semf", row_block, w_gate, preferred_element_type=jnp.float32)
    up_part = jnp.einsum("semd,edf->semf", row_block, w_up, preferred_element_type=jnp.float32)
    hidden = (jax.nn.silu(gate_part) * up_part).astype(jnp.bfloat16)
    result = jnp.einsum("semf,efd->semd", hidden, w_down, preferred_element_type=jnp.float32)
    return result.astype(jnp.bfloat16).reshape(array_shape)


def dispatch_matrix(slot_place, slot_total):
    slot_index = jnp.arange(slot_total, dtype=jnp.int32)
    matches = slot_index[:, None, None] == slot_place[None, :, :]
    return jnp.sum(matches.astype(jnp.int32), axis=2).astype(jnp.bfloat16)


def tile_rows(count):
    return -(-count // 16) * 16


def stage_order(step, place, length):
    if step == length - 1:
        return place
    down = length - 1 - step
    down = down - jnp.where(down <= place, 1, 0)
    up = step + jnp.where(place <= step, 1, 0)
    return jnp.where(place < length // 2, down, up)


def exchange_kernel(
    n,
    fp,
    x_ref,
    meta_ref,
    wsend_ref,
    eg_hbm,
    eu_hbm,
    ed_hbm,
    out_ref,
    xg,
    mg,
    w,
    eg,
    eu,
    ed,
    rows,
    exs,
    mid,
    rw,
    hid,
    csend,
    crecv,
    keep,
    ysend,
    yrecv,
    zsend,
    zrecv,
    load_sem,
    x_send,
    x_recv,
    m_send,
    m_recv,
    w_send,
    w_recv,
    c_send,
    c_recv,
    y_send,
    y_recv,
    z_send,
    z_recv,
):
    length = n // 4
    me = lax.axis_index("expert")
    z, y, c = me // 4, (me // 2) % 2, me % 2
    tokens, width = x_ref.shape
    per_block = rows.shape[0] // n
    part = w.shape[1] // n
    ff = eg.shape[1]
    bf16 = jnp.bfloat16

    def place(zz, yy, cc):
        return zz * 4 + yy * 2 + cc

    right, left = place(z + 1, y, c), place(z - 1, y, c)
    across, sibling = place(z, 1 - y, c), place(z, y, 1 - c)

    loads = [
        pltpu.make_async_copy(src, dst, load_sem.at[i])
        for i, (src, dst) in enumerate(((eg_hbm, eg), (eu_hbm, eu), (ed_hbm, ed)))
    ]
    for load in loads:
        load.start()

    barrier = pltpu.get_barrier_semaphore()
    for step in range(1, n):
        pl.semaphore_signal(
            barrier, inc=1, device_id={"expert": lax.rem(me + step, n)}, device_id_type=MESH
        )
    xg[me] = x_ref[...]
    mg[me] = meta_ref[...]
    pl.semaphore_wait(barrier, n - 1)

    def remote(src, dst, send, recv, target):
        return pltpu.make_async_remote_copy(
            src_ref=src,
            dst_ref=dst,
            send_sem=send,
            recv_sem=recv,
            device_id={"expert": target},
            device_id_type=MESH,
        )

    def block_copies(which, way, target):
        return (
            remote(xg.at[which], xg.at[which], x_send.at[way, which], x_recv.at[which], target),
            remote(mg.at[which], mg.at[which], m_send.at[way, which], m_recv.at[which], target),
        )

    def send_block(which, way, target):
        for copy in block_copies(which, way, target):
            copy.start()

    def sent_block(which, way, target):
        for copy in block_copies(which, way, target):
            copy.wait_send()

    def got_block(which):
        for copy in block_copies(which, 0, sibling):
            copy.wait_recv()

    def weight_copy(step):
        target = lax.rem(me + step, n)
        return remote(
            wsend_ref.at[target],
            w.at[:, pl.ds(pl.multiple_of(me * part, part), part)],
            w_send.at[step],
            w_recv.at[me],
            target,
        )

    def gate_block(which):
        token_block = xg[which]
        info = mg[which]
        spot = lax.broadcasted_iota(jnp.int32, (per_block, tokens), 0).astype(jnp.float32)
        base = (me * per_block).astype(jnp.float32)
        first = spot == info[0:1, :] - base
        second = spot == info[1:2, :] - base
        pick = jnp.where(first | second, 1.0, 0.0).astype(bf16)
        scale = jnp.where(first, info[2:3, :], 0.0) + jnp.where(second, info[3:4, :], 0.0)
        spots = pl.ds(pl.multiple_of(which * per_block, per_block), per_block)
        rows[spots, :] = jnp.dot(pick, token_block, preferred_element_type=jnp.float32).astype(bf16)
        rw[spots, :] = jnp.broadcast_to(jnp.sum(scale, axis=1, keepdims=True), (per_block, 128))
        both = lax.dot_general(
            token_block, w[0 : 2 * fp, :], (((1,), (1,)), ((), ())), preferred_element_type=jnp.float32
        )
        gate, up = both[:, :fp], both[:, fp:]
        hid[which] = (gate * jax.nn.sigmoid(gate) * up).astype(bf16)

    def group(zz, index):
        return place(zz, (y + index // 2) % 2, (c + index % 2) % 2)

    for step in range(length + 1):
        if step < length:
            zs = stage_order(length - 1 - step, z, length)
            which = place(zs, y, c)
            if step > 0:
                got_block(which)

            @pl.when((zs <= z) & (z < length - 1))
            def _():
                send_block(which, 0, right)

            @pl.when((zs >= z) & (z > 0))
            def _():
                send_block(which, 1, left)

            send_block(which, 2, across)
            send_block(which, 3, sibling)
        if step == 0:
            for other in range(1, n):
                weight_copy(other).start()
            w[:, pl.ds(pl.multiple_of(me * part, part), part)] = wsend_ref[me]
        else:
            zp = stage_order(length - step, z, length)
            far = place(zp, 1 - y, c)
            got_block(far)
            send_block(far, 3, sibling)
            got_block(place(zp, y, 1 - c))
            got_block(place(zp, 1 - y, 1 - c))
            if step == 1:
                for other in range(1, n):
                    source = lax.rem(me + other, n)
                    remote(
                        wsend_ref.at[0],
                        w.at[:, pl.ds(pl.multiple_of(source * part, part), part)],
                        w_send.at[other],
                        w_recv.at[source],
                        source,
                    ).wait_recv()

            def one_block(index, carry):
                gate_block(group(zp, index))
                return carry

            lax.fori_loop(0, 4, one_block, 0)

    for load in loads:
        load.wait()
    chunk = rows.shape[0] // 2
    tile = ff // 3 if ff % 384 == 0 else ff

    def expert_chunk(index, carry):
        spots = pl.ds(pl.multiple_of(index * chunk, chunk), chunk)

        def hidden_tile(at, inner):
            columns = pl.ds(pl.multiple_of(at * tile, 128), tile)
            taken = rows[spots, :]
            gate = jnp.dot(taken, eg[:, columns], preferred_element_type=jnp.float32)
            up = jnp.dot(taken, eu[:, columns], preferred_element_type=jnp.float32)
            mid[:, columns] = (gate * jax.nn.sigmoid(gate) * up).astype(bf16)
            return inner

        lax.fori_loop(0, ff // tile, hidden_tile, 0)

        def out_tile(at, inner):
            columns = pl.ds(pl.multiple_of(at * 512, 512), 512)
            result = jnp.dot(mid[...], ed[:, columns], preferred_element_type=jnp.float32)
            exs[spots, columns] = (result * rw[spots, 0:1]).astype(bf16)
            return inner

        lax.fori_loop(0, width // 512, out_tile, 0)
        return carry

    lax.fori_loop(0, 2, expert_chunk, 0)

    def partial_sum(which):
        info = mg[which]
        spot = lax.broadcasted_iota(jnp.int32, (per_block, tokens), 0).astype(jnp.float32)
        base = (me * per_block).astype(jnp.float32)
        pick = jnp.where(
            (spot == info[0:1, :] - base) | (spot == info[1:2, :] - base), 1.0, 0.0
        ).astype(bf16)
        spots = pl.ds(pl.multiple_of(which * per_block, per_block), per_block)
        routed = lax.dot_general(
            pick, exs[spots, :], (((0,), (0,)), ((), ())), preferred_element_type=jnp.float32
        )
        return routed + jnp.dot(
            hid[which], w[2 * fp : 3 * fp, :], preferred_element_type=jnp.float32
        )

    def core_copy(zz, yy):
        at = yy * length + zz
        return remote(csend.at[at], crecv.at[at], c_send.at[at], c_recv.at[at], sibling)

    def y_copy(zz):
        return remote(ysend.at[zz], yrecv.at[zz], y_send.at[zz], y_recv.at[zz], across)

    def z_copy(way, zz, target):
        return remote(zsend.at[zz], zrecv.at[way, zz], z_send.at[zz], z_recv.at[way, zz], target)

    for step in range(length + 1):
        if step < length:
            zs = stage_order(step, z, length)
            for yy in (1 - y, y):
                csend[yy * length + zs] = partial_sum(place(zs, yy, 1 - c)).astype(bf16)
                core_copy(zs, yy).start()
            keep[zs] = partial_sum(place(zs, 1 - y, c))
            core_copy(zs, 1 - y).wait_recv()
            ysend[zs] = (keep[zs] + crecv[(1 - y) * length + zs].astype(jnp.float32)).astype(bf16)
            y_copy(zs).start()
            keep[zs] = partial_sum(place(zs, y, c))
            core_copy(zs, y).wait_recv()
            keep[zs] += crecv[y * length + zs].astype(jnp.float32)
        if step > 0:
            zp = stage_order(step - 1, z, length)
            y_copy(zp).wait_recv()
            keep[zp] += yrecv[zp].astype(jnp.float32)

            @pl.when((zp >= z) & (z > 0))
            def _():
                z_copy(0, zp, left).wait_recv()
                keep[zp] += zrecv[0, zp].astype(jnp.float32)

            @pl.when((zp <= z) & (z < length - 1))
            def _():
                z_copy(1, zp, right).wait_recv()
                keep[zp] += zrecv[1, zp].astype(jnp.float32)

            if step < length:
                zsend[zp] = keep[zp].astype(bf16)

                @pl.when(zp > z)
                def _():
                    z_copy(0, zp, right).start()

                @pl.when(zp < z)
                def _():
                    z_copy(1, zp, left).start()

    out_ref[...] = keep[z]

    for step in range(length):
        zs = stage_order(step, z, length)
        which = place(zs, y, c)

        @pl.when((zs <= z) & (z < length - 1))
        def _():
            sent_block(which, 0, right)

        @pl.when((zs >= z) & (z > 0))
        def _():
            sent_block(which, 1, left)

        sent_block(which, 2, across)
        sent_block(which, 3, sibling)
        sent_block(place(zs, 1 - y, c), 3, sibling)
        core_copy(zs, 1 - y).wait_send()
        core_copy(zs, y).wait_send()
        y_copy(zs).wait_send()
        if step < length - 1:

            @pl.when(zs > z)
            def _():
                z_copy(0, zs, right).wait_send()

            @pl.when(zs < z)
            def _():
                z_copy(1, zs, left).wait_send()

    for other in range(1, n):
        weight_copy(other).wait_send()


def exchange(n, fp, slots, flat_rows, meta, wsend, w_gate, w_up, w_down):
    length = n // 4
    tokens, width = flat_rows.shape
    ff = w_gate.shape[1]
    bf16, f32 = jnp.bfloat16, jnp.float32
    whole = pl.BlockSpec(memory_space=pltpu.VMEM)
    away = pl.BlockSpec(memory_space=pl.ANY)
    sems = pltpu.SemaphoreType.DMA
    return pl.pallas_call(
        functools.partial(exchange_kernel, n, fp),
        out_shape=jax.ShapeDtypeStruct((tokens, width), f32),
        in_specs=[whole, whole, whole, away, away, away],
        out_specs=whole,
        scratch_shapes=[
            pltpu.VMEM((n, tokens, width), bf16),
            pltpu.VMEM((n,) + meta.shape, f32),
            pltpu.VMEM((3 * fp, width), bf16),
            pltpu.VMEM((width, ff), bf16),
            pltpu.VMEM((width, ff), bf16),
            pltpu.VMEM((ff, width), bf16),
            pltpu.VMEM((n * slots, width), bf16),
            pltpu.VMEM((n * slots, width), bf16),
            pltpu.VMEM((n * slots // 2, ff), bf16),
            pltpu.VMEM((n * slots, 128), f32),
            pltpu.VMEM((n, tokens, fp), bf16),
            pltpu.VMEM((2 * length, tokens, width), bf16),
            pltpu.VMEM((2 * length, tokens, width), bf16),
            pltpu.VMEM((length, tokens, width), f32),
            pltpu.VMEM((length, tokens, width), bf16),
            pltpu.VMEM((length, tokens, width), bf16),
            pltpu.VMEM((length, tokens, width), bf16),
            pltpu.VMEM((2, length, tokens, width), bf16),
            sems((3,)),
            sems((4, n)),
            sems((n,)),
            sems((4, n)),
            sems((n,)),
            sems((n,)),
            sems((n,)),
            sems((2 * length,)),
            sems((2 * length,)),
            sems((length,)),
            sems((length,)),
            sems((length,)),
            sems((2, length)),
        ],
        compiler_params=pltpu.CompilerParams(
            collective_id=0, has_side_effects=True, vmem_limit_bytes=60 * 1024 * 1024
        ),
    )(flat_rows, meta, wsend, w_gate, w_up, w_down)


def fits(n, tokens, width, slots, ff, local_count, experts):
    moved = n * tokens * width * 2 * 4
    weights = 3 * width * ff * 2 + 2 * n * slots * width * 2
    return (
        n % 4 == 0
        and experts == n
        and local_count == 1
        and tokens == 128
        and width % (n * 128) == 0
        and width % 512 == 0
        and ff % 128 == 0
        and slots % 16 == 0
        and moved + weights < 56 * 1024 * 1024
    )


def local(
    n,
    tokens,
    route_ids,
    route_slots,
    mod_shift,
    mod_scale,
    mod_gate,
    guidance,
    router_weight,
    expert_gate,
    expert_up,
    expert_down,
    shared_gate,
    shared_up,
    shared_down,
    head_weight,
):
    model_width = tokens.shape[-1]
    per_half = tokens.shape[1]
    choices_each = route_ids.shape[2]
    experts = router_weight.shape[1]
    capacity = 2 * choices_each * per_half // experts
    inputs = tokens.astype(jnp.float32)
    modulated = (layer_norm(inputs) * (1.0 + mod_scale[:, None, :]) + mod_shift[:, None, :]).astype(
        jnp.bfloat16
    )
    flat_rows = modulated.reshape(2 * per_half, model_width)
    logits = jnp.dot(flat_rows, router_weight, preferred_element_type=jnp.float32).reshape(
        2, per_half, experts
    )
    picked = jnp.take_along_axis(logits, route_ids, axis=2)
    affinity = jax.nn.sigmoid(picked)
    weights = affinity / jnp.sum(affinity, axis=2, keepdims=True)
    half_index = jnp.arange(2, dtype=jnp.int32)
    slot_place = (route_ids * 2 + half_index[:, None, None]) * capacity + route_slots
    slots = 2 * capacity
    if choices_each == 2 and fits(
        n,
        2 * per_half,
        model_width,
        slots,
        expert_gate.shape[2],
        expert_gate.shape[0],
        experts,
    ):
        share = shared_gate.shape[1] // n
        fp = tile_rows(share)
        pieces = [
            jnp.pad(piece.reshape(n, share, -1), ((0, 0), (0, fp - share), (0, 0)))
            for piece in (shared_gate.T, shared_up.T, shared_down)
        ]
        wsend = jnp.concatenate(pieces, axis=1)
        flat_place = slot_place.reshape(2 * per_half, choices_each).astype(jnp.float32)
        flat_weight = weights.reshape(2 * per_half, choices_each)
        meta = jnp.concatenate([flat_place, flat_weight], axis=1).T
        meta = jnp.pad(meta, ((0, 8 - meta.shape[0]), (0, 0)))
        added = exchange(
            n, fp, slots, flat_rows, meta, wsend, expert_gate[0], expert_up[0], expert_down[0]
        ).reshape(2, per_half, model_width)
    else:
        full_gate, full_up, full_down = (
            lax.all_gather(shared_gate, "expert", axis=0, tiled=True),
            lax.all_gather(shared_up, "expert", axis=0, tiled=True),
            lax.all_gather(shared_down, "expert", axis=1, tiled=True),
        )
        gate_sum = jnp.dot(flat_rows, full_gate, preferred_element_type=jnp.float32)
        up_sum = jnp.dot(flat_rows, full_up, preferred_element_type=jnp.float32)
        shared_hidden = (jax.nn.silu(gate_sum) * up_sum).astype(jnp.bfloat16)
        shared = jnp.dot(shared_hidden, full_down, preferred_element_type=jnp.float32)
        shared = shared.reshape(2, per_half, model_width)
        matrix = dispatch_matrix(slot_place.reshape(2 * per_half, choices_each), 2 * experts * capacity)
        outgoing = jnp.dot(matrix, flat_rows, preferred_element_type=jnp.float32).astype(jnp.bfloat16)
        outgoing = outgoing.reshape(experts, 2, capacity, model_width)
        answered = expert_block(
            lax.all_to_all(outgoing, "expert", split_axis=0, concat_axis=0, tiled=True),
            expert_gate,
            expert_up,
            expert_down,
        )
        returned = lax.all_to_all(answered, "expert", split_axis=0, concat_axis=0, tiled=True)
        chosen = jnp.take(returned.reshape(-1, model_width), slot_place.reshape(-1), axis=0)
        chosen = chosen.reshape(2, per_half, choices_each, model_width)
        routed = jnp.sum(weights[..., None] * chosen.astype(jnp.float32), axis=2)
        added = routed + shared
    hidden_out = (inputs + mod_gate[:, None, :] * added).astype(jnp.bfloat16)
    final_norm = layer_norm(hidden_out.astype(jnp.float32)).astype(jnp.bfloat16)
    predicted = jnp.dot(
        final_norm.reshape(2 * per_half, model_width),
        head_weight,
        preferred_element_type=jnp.float32,
    )
    predicted = predicted.reshape(2, per_half, head_weight.shape[1])
    guided = predicted[1] + guidance[0] * (predicted[0] - predicted[1])
    return (hidden_out, guided)


def solution(mesh):
    in_specs = (
        P(None, ("groups", "expert"), None),
        P(None, ("groups", "expert"), None),
        P(None, ("groups", "expert"), None),
        P("groups", None),
        P("groups", None),
        P("groups", None),
        P("groups"),
        P(),
        P("expert", None, None),
        P("expert", None, None),
        P("expert", None, None),
        P("expert", None),
        P("expert", None),
        P(None, "expert"),
        P(),
    )
    out_specs = (P(None, ("groups", "expert"), None), P(("groups", "expert"), None))
    run = functools.partial(local, mesh.shape["expert"])
    return jax.shard_map(run, mesh=mesh, in_specs=in_specs, out_specs=out_specs, check_vma=False)
```

```python
import functools
import math

import jax
import jax.numpy as jnp
from jax import lax
from jax.experimental import pallas as pl
from jax.experimental.pallas import tpu as pltpu
from jax.sharding import PartitionSpec as P

epsilon = 1e-06
MESH = pl.DeviceIdType.MESH


def layer_norm(values):
    center = values - jnp.mean(values, axis=-1, keepdims=True)
    spread = jnp.mean(center * center, axis=-1, keepdims=True)
    return center * lax.rsqrt(spread + epsilon)


def expert_block(received, w_gate, w_up, w_down):
    array_shape = received.shape
    local_count = w_gate.shape[0]
    middle = math.prod(array_shape[1:-1])
    row_block = received.reshape(
        array_shape[0] // local_count, local_count, middle, array_shape[-1]
    )
    gate_part = jnp.einsum("semd,edf->semf", row_block, w_gate, preferred_element_type=jnp.float32)
    up_part = jnp.einsum("semd,edf->semf", row_block, w_up, preferred_element_type=jnp.float32)
    hidden = (jax.nn.silu(gate_part) * up_part).astype(jnp.bfloat16)
    result = jnp.einsum("semf,efd->semd", hidden, w_down, preferred_element_type=jnp.float32)
    return result.astype(jnp.bfloat16).reshape(array_shape)


def dispatch_matrix(slot_place, slot_total):
    slot_index = jnp.arange(slot_total, dtype=jnp.int32)
    matches = slot_index[:, None, None] == slot_place[None, :, :]
    return jnp.sum(matches.astype(jnp.int32), axis=2).astype(jnp.bfloat16)


def tile_rows(count):
    return -(-count // 16) * 16


def stage_order(step, place, length):
    if step == length - 1:
        return place
    down = length - 1 - step
    down = down - jnp.where(down <= place, 1, 0)
    up = step + jnp.where(place <= step, 1, 0)
    return jnp.where(place < length // 2, down, up)


def exchange_kernel(
    n,
    spread,
    fp,
    x_ref,
    meta_ref,
    wsend_ref,
    eg_hbm,
    eu_hbm,
    ed_hbm,
    out_ref,
    xg,
    mg,
    w,
    eg,
    eu,
    ed,
    rows,
    exs,
    mid,
    rw,
    hid,
    csend,
    crecv,
    keep,
    ysend,
    yrecv,
    zsend,
    zrecv,
    load_sem,
    x_send,
    x_recv,
    m_send,
    m_recv,
    w_send,
    w_recv,
    c_send,
    c_recv,
    y_send,
    y_recv,
    z_send,
    z_recv,
    h_send,
    h_recv,
):
    length = n // 4
    me = lax.axis_index("expert")
    z, y, c = me // 4, (me // 2) % 2, me % 2
    tokens, width = x_ref.shape
    per_block = rows.shape[0] // n
    part = w.shape[1] // n
    ff = eg.shape[1]
    bf16 = jnp.bfloat16

    def block(which):
        return pl.ds(pl.multiple_of(which * tokens, tokens), tokens)

    def place(zz, yy, cc):
        return zz * 4 + yy * 2 + cc

    right, left = place(z + 1, y, c), place(z - 1, y, c)
    across, sibling = place(z, 1 - y, c), place(z, y, 1 - c)

    loads = [
        pltpu.make_async_copy(src, dst, load_sem.at[i])
        for i, (src, dst) in enumerate(((eg_hbm, eg), (eu_hbm, eu), (ed_hbm, ed)))
    ]
    for load in loads:
        load.start()

    barrier = pltpu.get_barrier_semaphore()
    for step in range(1, n):
        pl.semaphore_signal(
            barrier, inc=1, device_id={"expert": lax.rem(me + step, n)}, device_id_type=MESH
        )
    group_at = lax.axis_index("groups")
    for other in range(1, spread):
        pl.semaphore_signal(
            barrier,
            inc=1,
            device_id={"groups": lax.rem(group_at + other, spread)},
            device_id_type=MESH,
        )
    xg[block(me), :] = x_ref[...]
    mg[me] = meta_ref[...]
    pl.semaphore_wait(barrier, n - 1 + spread - 1)

    def remote(src, dst, send, recv, target):
        return pltpu.make_async_remote_copy(
            src_ref=src,
            dst_ref=dst,
            send_sem=send,
            recv_sem=recv,
            device_id={"expert": target},
            device_id_type=MESH,
        )

    def block_copies(which, way, target):
        return (
            remote(xg.at[block(which)], xg.at[block(which)], x_send.at[way, which], x_recv.at[which], target),
            remote(mg.at[which], mg.at[which], m_send.at[way, which], m_recv.at[which], target),
        )

    def send_block(which, way, target):
        for copy in block_copies(which, way, target):
            copy.start()

    def sent_block(which, way, target):
        for copy in block_copies(which, way, target):
            copy.wait_send()

    def got_block(which):
        for copy in block_copies(which, 0, sibling):
            copy.wait_recv()

    share = w.shape[0] // spread
    own_share = pl.ds(pl.multiple_of(lax.rem(group_at, spread) * share, share), share)

    def weight_columns(source):
        return pl.ds(pl.multiple_of(source * part, part), part)

    def weight_copy(step):
        target = lax.rem(me + step, n)
        return remote(
            wsend_ref.at[target, own_share],
            w.at[own_share, weight_columns(me)],
            w_send.at[step],
            w_recv.at[me],
            target,
        )

    def weight_landing(step):
        source = lax.rem(me + step, n)
        return remote(
            wsend_ref.at[source, own_share],
            w.at[own_share, weight_columns(source)],
            w_send.at[step],
            w_recv.at[source],
            source,
        )

    def hand_on(step):
        return pltpu.make_async_remote_copy(
            src_ref=w.at[own_share],
            dst_ref=w.at[own_share],
            send_sem=h_send.at[step],
            recv_sem=h_recv.at[step],
            device_id={"groups": lax.rem(group_at + step, spread)},
            device_id_type=MESH,
        )

    def route_rows(which):
        info = mg[which]
        spot = lax.broadcasted_iota(jnp.int32, (per_block, tokens), 0).astype(jnp.float32)
        base = (me * per_block).astype(jnp.float32)
        first = spot == info[0:1, :] - base
        second = spot == info[1:2, :] - base
        pick = jnp.where(first | second, 1.0, 0.0).astype(bf16)
        scale = jnp.where(first, info[2:3, :], 0.0) + jnp.where(second, info[3:4, :], 0.0)
        spots = pl.ds(pl.multiple_of(which * per_block, per_block), per_block)
        rows[spots, :] = jnp.dot(
            pick, xg[block(which), :], preferred_element_type=jnp.float32
        ).astype(bf16)
        rw[spots, :] = jnp.broadcast_to(jnp.sum(scale, axis=1, keepdims=True), (per_block, 128))

    chunk = 4 * per_block
    tile = ff // 3 if ff % 384 == 0 else ff

    def expert_group(zz):
        def one_block(index, carry):
            route_rows(zz * 4 + index)
            return carry

        lax.fori_loop(0, 4, one_block, 0)
        spots = pl.ds(pl.multiple_of(zz * chunk, chunk), chunk)

        def hidden_tile(at, inner):
            columns = pl.ds(pl.multiple_of(at * tile, 128), tile)
            taken = rows[spots, :]
            gate = jnp.dot(taken, eg[:, columns], preferred_element_type=jnp.float32)
            up = jnp.dot(taken, eu[:, columns], preferred_element_type=jnp.float32)
            mid[:, columns] = (gate * jax.nn.sigmoid(gate) * up).astype(bf16)
            return inner

        lax.fori_loop(0, ff // tile, hidden_tile, 0)

        def out_tile(at, inner):
            columns = pl.ds(pl.multiple_of(at * 512, 512), 512)
            result = jnp.dot(mid[...], ed[:, columns], preferred_element_type=jnp.float32)
            exs[spots, columns] = (result * rw[spots, 0:1]).astype(bf16)
            return inner

        lax.fori_loop(0, width // 512, out_tile, 0)

    def shared_group(zz):
        spots = pl.ds(pl.multiple_of(zz * 4 * tokens, tokens), 4 * tokens)
        both = lax.dot_general(
            xg[spots, :], w[0 : 2 * fp, :], (((1,), (1,)), ((), ())), preferred_element_type=jnp.float32
        )
        gate, up = both[:, :fp], both[:, fp:]
        hid[spots, :] = (gate * jax.nn.sigmoid(gate) * up).astype(bf16)

    def partial_sum(which):
        info = mg[which]
        spot = lax.broadcasted_iota(jnp.int32, (per_block, tokens), 0).astype(jnp.float32)
        base = (me * per_block).astype(jnp.float32)
        pick = jnp.where(
            (spot == info[0:1, :] - base) | (spot == info[1:2, :] - base), 1.0, 0.0
        ).astype(bf16)
        spots = pl.ds(pl.multiple_of(which * per_block, per_block), per_block)
        routed = lax.dot_general(
            pick, exs[spots, :], (((0,), (0,)), ((), ())), preferred_element_type=jnp.float32
        )
        return routed + jnp.dot(
            hid[block(which), :], w[2 * fp : 3 * fp, :], preferred_element_type=jnp.float32
        )

    def core_copy(zz, yy):
        at = yy * length + zz
        return remote(csend.at[at], crecv.at[at], c_send.at[at], c_recv.at[at], sibling)

    def y_copy(zz):
        return remote(ysend.at[zz], yrecv.at[zz], y_send.at[zz], y_recv.at[zz], across)

    def z_copy(way, zz, target):
        return remote(zsend.at[zz], zrecv.at[way, zz], z_send.at[zz], z_recv.at[way, zz], target)

    def y_step(step):
        zs = stage_order(step, z, length)
        for yy in (1 - y, y):
            csend[yy * length + zs] = partial_sum(place(zs, yy, 1 - c)).astype(bf16)
            core_copy(zs, yy).start()
        keep[zs] = partial_sum(place(zs, 1 - y, c))
        core_copy(zs, 1 - y).wait_recv()
        ysend[zs] = (keep[zs] + crecv[(1 - y) * length + zs].astype(jnp.float32)).astype(bf16)
        y_copy(zs).start()
        keep[zs] = partial_sum(place(zs, y, c))
        core_copy(zs, y).wait_recv()
        keep[zs] += crecv[y * length + zs].astype(jnp.float32)

    def z_step(step):
        zp = stage_order(step, z, length)
        y_copy(zp).wait_recv()
        keep[zp] += yrecv[zp].astype(jnp.float32)

        @pl.when((zp >= z) & (z > 0))
        def _():
            z_copy(0, zp, left).wait_recv()
            keep[zp] += zrecv[0, zp].astype(jnp.float32)

        @pl.when((zp <= z) & (z < length - 1))
        def _():
            z_copy(1, zp, right).wait_recv()
            keep[zp] += zrecv[1, zp].astype(jnp.float32)

        if step < length - 1:
            zsend[zp] = keep[zp].astype(bf16)

            @pl.when(zp > z)
            def _():
                z_copy(0, zp, right).start()

            @pl.when(zp < z)
            def _():
                z_copy(1, zp, left).start()

    def arrival(step):
        return stage_order(length - 1 - step, z, length)

    early = length - 2
    for step in range(length + 1):
        if step < length:
            zs = arrival(step)
            which = place(zs, y, c)
            if step > 0:
                got_block(which)

            @pl.when((zs <= z) & (z < length - 1))
            def _():
                send_block(which, 0, right)

            @pl.when((zs >= z) & (z > 0))
            def _():
                send_block(which, 1, left)

            send_block(which, 2, across)
            send_block(which, 3, sibling)
        if step == 0:
            for other in range(1, n):
                weight_copy(other).start()
            w[own_share, weight_columns(me)] = wsend_ref[me, own_share]
            for load in loads:
                load.wait()
            continue
        zp = arrival(step - 1)
        far = place(zp, 1 - y, c)
        got_block(far)
        send_block(far, 3, sibling)
        got_block(place(zp, y, 1 - c))
        got_block(place(zp, 1 - y, 1 - c))
        expert_group(zp)
        if step == 1:
            for other in range(1, n):
                weight_landing(other).wait_recv()
            for other in range(1, spread):
                hand_on(other).start()
        if step == length - 1:
            for other in range(1, spread):
                landed = lax.rem(group_at + spread - other, spread) * share
                landed = pl.ds(pl.multiple_of(landed, share), share)
                pltpu.make_async_remote_copy(
                    src_ref=w.at[landed],
                    dst_ref=w.at[landed],
                    send_sem=h_send.at[other],
                    recv_sem=h_recv.at[other],
                    device_id={"groups": lax.rem(group_at + other, spread)},
                    device_id_type=MESH,
                ).wait_recv()
            for done in range(length - 1):
                shared_group(arrival(done))
            y_step(early)
        if step == length:
            shared_group(zp)

    later = [step for step in range(length) if step != early]
    y_step(later[0])
    sent = 0
    for step in later[1:]:
        y_step(step)
        z_step(sent)
        sent += 1
    for step in range(sent, length):
        z_step(step)

    out_ref[...] = keep[z]

    for step in range(length):
        zs = stage_order(step, z, length)
        which = place(zs, y, c)

        @pl.when((zs <= z) & (z < length - 1))
        def _():
            sent_block(which, 0, right)

        @pl.when((zs >= z) & (z > 0))
        def _():
            sent_block(which, 1, left)

        sent_block(which, 2, across)
        sent_block(which, 3, sibling)
        sent_block(place(zs, 1 - y, c), 3, sibling)
        core_copy(zs, 1 - y).wait_send()
        core_copy(zs, y).wait_send()
        y_copy(zs).wait_send()
        if step < length - 1:

            @pl.when(zs > z)
            def _():
                z_copy(0, zs, right).wait_send()

            @pl.when(zs < z)
            def _():
                z_copy(1, zs, left).wait_send()

    for other in range(1, n):
        weight_copy(other).wait_send()
    for other in range(1, spread):
        hand_on(other).wait_send()


def exchange(n, spread, fp, slots, flat_rows, meta, wsend, w_gate, w_up, w_down):
    length = n // 4
    tokens, width = flat_rows.shape
    ff = w_gate.shape[1]
    bf16, f32 = jnp.bfloat16, jnp.float32
    whole = pl.BlockSpec(memory_space=pltpu.VMEM)
    away = pl.BlockSpec(memory_space=pl.ANY)
    sems = pltpu.SemaphoreType.DMA
    return pl.pallas_call(
        functools.partial(exchange_kernel, n, spread, fp),
        out_shape=jax.ShapeDtypeStruct((tokens, width), f32),
        in_specs=[whole, whole, whole, away, away, away],
        out_specs=whole,
        scratch_shapes=[
            pltpu.VMEM((n * tokens, width), bf16),
            pltpu.VMEM((n,) + meta.shape, f32),
            pltpu.VMEM((3 * fp, width), bf16),
            pltpu.VMEM((width, ff), bf16),
            pltpu.VMEM((width, ff), bf16),
            pltpu.VMEM((ff, width), bf16),
            pltpu.VMEM((n * slots, width), bf16),
            pltpu.VMEM((n * slots, width), bf16),
            pltpu.VMEM((4 * slots, ff), bf16),
            pltpu.VMEM((n * slots, 128), f32),
            pltpu.VMEM((n * tokens, fp), bf16),
            pltpu.VMEM((2 * length, tokens, width), bf16),
            pltpu.VMEM((2 * length, tokens, width), bf16),
            pltpu.VMEM((length, tokens, width), f32),
            pltpu.VMEM((length, tokens, width), bf16),
            pltpu.VMEM((length, tokens, width), bf16),
            pltpu.VMEM((length, tokens, width), bf16),
            pltpu.VMEM((2, length, tokens, width), bf16),
            sems((3,)),
            sems((4, n)),
            sems((n,)),
            sems((4, n)),
            sems((n,)),
            sems((n,)),
            sems((n,)),
            sems((2 * length,)),
            sems((2 * length,)),
            sems((length,)),
            sems((length,)),
            sems((length,)),
            sems((2, length)),
            sems((spread,)),
            sems((spread,)),
        ],
        compiler_params=pltpu.CompilerParams(
            collective_id=0, has_side_effects=True, vmem_limit_bytes=60 * 1024 * 1024
        ),
    )(flat_rows, meta, wsend, w_gate, w_up, w_down)


def fits(n, tokens, width, slots, ff, local_count, experts):
    moved = n * tokens * width * 2 * 4
    weights = 3 * width * ff * 2 + 2 * n * slots * width * 2
    return (
        n % 4 == 0
        and n > 8
        and experts == n
        and local_count == 1
        and tokens == 128
        and width % (n * 128) == 0
        and width % 512 == 0
        and ff % 128 == 0
        and slots % 16 == 0
        and moved + weights < 56 * 1024 * 1024
    )


def local(
    n,
    parts,
    tokens,
    route_ids,
    route_slots,
    mod_shift,
    mod_scale,
    mod_gate,
    guidance,
    router_weight,
    expert_gate,
    expert_up,
    expert_down,
    shared_gate,
    shared_up,
    shared_down,
    head_weight,
):
    model_width = tokens.shape[-1]
    per_half = tokens.shape[1]
    choices_each = route_ids.shape[2]
    experts = router_weight.shape[1]
    capacity = 2 * choices_each * per_half // experts
    inputs = tokens.astype(jnp.float32)
    modulated = (layer_norm(inputs) * (1.0 + mod_scale[:, None, :]) + mod_shift[:, None, :]).astype(
        jnp.bfloat16
    )
    flat_rows = modulated.reshape(2 * per_half, model_width)
    logits = jnp.dot(flat_rows, router_weight, preferred_element_type=jnp.float32).reshape(
        2, per_half, experts
    )
    chosen_expert = route_ids[..., None] == jnp.arange(experts, dtype=jnp.int32)
    picked = jnp.sum(jnp.where(chosen_expert, logits[:, :, None, :], 0.0), axis=3)
    affinity = jax.nn.sigmoid(picked)
    weights = affinity / jnp.sum(affinity, axis=2, keepdims=True)
    half_index = jnp.arange(2, dtype=jnp.int32)
    slot_place = (route_ids * 2 + half_index[:, None, None]) * capacity + route_slots
    slots = 2 * capacity
    if choices_each == 2 and fits(
        n,
        2 * per_half,
        model_width,
        slots,
        expert_gate.shape[2],
        expert_gate.shape[0],
        experts,
    ):
        share = shared_gate.shape[1] // n
        fp = tile_rows(share)
        spread = parts if 3 * fp % (16 * parts) == 0 else 1
        pieces = [
            jnp.pad(piece.reshape(n, share, -1), ((0, 0), (0, fp - share), (0, 0)))
            for piece in (shared_gate.T, shared_up.T, shared_down)
        ]
        wsend = jnp.concatenate(pieces, axis=1)
        flat_place = slot_place.reshape(2 * per_half, choices_each).astype(jnp.float32)
        flat_weight = weights.reshape(2 * per_half, choices_each)
        meta = jnp.concatenate([flat_place, flat_weight], axis=1).T
        meta = jnp.pad(meta, ((0, 8 - meta.shape[0]), (0, 0)))
        added = exchange(
            n, spread, fp, slots, flat_rows, meta, wsend, expert_gate[0], expert_up[0], expert_down[0]
        ).reshape(2, per_half, model_width)
    else:
        full_gate, full_up, full_down = (
            lax.all_gather(shared_gate, "expert", axis=0, tiled=True),
            lax.all_gather(shared_up, "expert", axis=0, tiled=True),
            lax.all_gather(shared_down, "expert", axis=1, tiled=True),
        )
        gate_sum = jnp.dot(flat_rows, full_gate, preferred_element_type=jnp.float32)
        up_sum = jnp.dot(flat_rows, full_up, preferred_element_type=jnp.float32)
        shared_hidden = (jax.nn.silu(gate_sum) * up_sum).astype(jnp.bfloat16)
        shared = jnp.dot(shared_hidden, full_down, preferred_element_type=jnp.float32)
        shared = shared.reshape(2, per_half, model_width)
        matrix = dispatch_matrix(slot_place.reshape(2 * per_half, choices_each), 2 * experts * capacity)
        outgoing = jnp.dot(matrix, flat_rows, preferred_element_type=jnp.float32).astype(jnp.bfloat16)
        outgoing = outgoing.reshape(experts, 2, capacity, model_width)
        answered = expert_block(
            lax.all_to_all(outgoing, "expert", split_axis=0, concat_axis=0, tiled=True),
            expert_gate,
            expert_up,
            expert_down,
        )
        returned = lax.all_to_all(answered, "expert", split_axis=0, concat_axis=0, tiled=True)
        chosen = jnp.take(returned.reshape(-1, model_width), slot_place.reshape(-1), axis=0)
        chosen = chosen.reshape(2, per_half, choices_each, model_width)
        routed = jnp.sum(weights[..., None] * chosen.astype(jnp.float32), axis=2)
        added = routed + shared
    hidden_out = (inputs + mod_gate[:, None, :] * added).astype(jnp.bfloat16)
    final_norm = layer_norm(hidden_out.astype(jnp.float32)).astype(jnp.bfloat16)
    predicted = jnp.dot(
        final_norm.reshape(2 * per_half, model_width),
        head_weight,
        preferred_element_type=jnp.float32,
    )
    predicted = predicted.reshape(2, per_half, head_weight.shape[1])
    guided = predicted[1] + guidance[0] * (predicted[0] - predicted[1])
    return (hidden_out, guided)


def solution(mesh):
    in_specs = (
        P(None, ("groups", "expert"), None),
        P(None, ("groups", "expert"), None),
        P(None, ("groups", "expert"), None),
        P("groups", None),
        P("groups", None),
        P("groups", None),
        P("groups"),
        P(),
        P("expert", None, None),
        P("expert", None, None),
        P("expert", None, None),
        P("expert", None),
        P("expert", None),
        P(None, "expert"),
        P(),
    )
    out_specs = (P(None, ("groups", "expert"), None), P(("groups", "expert"), None))
    run = functools.partial(local, mesh.shape["expert"], mesh.shape["groups"])
    return jax.shard_map(run, mesh=mesh, in_specs=in_specs, out_specs=out_specs, check_vma=False)
```

```python
import functools
import math

import jax
import jax.numpy as jnp
from jax import lax
from jax.experimental import pallas as pl
from jax.experimental.pallas import tpu as pltpu
from jax.sharding import PartitionSpec as P

epsilon = 1e-06
MESH = pl.DeviceIdType.MESH


def layer_norm(values):
    center = values - jnp.mean(values, axis=-1, keepdims=True)
    spread = jnp.mean(center * center, axis=-1, keepdims=True)
    return center * lax.rsqrt(spread + epsilon)


def expert_block(received, w_gate, w_up, w_down):
    array_shape = received.shape
    local_count = w_gate.shape[0]
    middle = math.prod(array_shape[1:-1])
    row_block = received.reshape(
        array_shape[0] // local_count, local_count, middle, array_shape[-1]
    )
    gate_part = jnp.einsum("semd,edf->semf", row_block, w_gate, preferred_element_type=jnp.float32)
    up_part = jnp.einsum("semd,edf->semf", row_block, w_up, preferred_element_type=jnp.float32)
    hidden = (jax.nn.silu(gate_part) * up_part).astype(jnp.bfloat16)
    result = jnp.einsum("semf,efd->semd", hidden, w_down, preferred_element_type=jnp.float32)
    return result.astype(jnp.bfloat16).reshape(array_shape)


def dispatch_matrix(slot_place, slot_total):
    slot_index = jnp.arange(slot_total, dtype=jnp.int32)
    matches = slot_index[:, None, None] == slot_place[None, :, :]
    return jnp.sum(matches.astype(jnp.int32), axis=2).astype(jnp.bfloat16)


def tile_rows(count):
    return -(-count // 16) * 16


def stage_order(step, place, length):
    if step == length - 1:
        return place
    down = length - 1 - step
    down = down - jnp.where(down <= place, 1, 0)
    up = step + jnp.where(place <= step, 1, 0)
    return jnp.where(place < length // 2, down, up)


def exchange_kernel(
    n,
    spread,
    fp,
    x_ref,
    meta_ref,
    wsend_ref,
    eg_hbm,
    eu_hbm,
    ed_hbm,
    out_ref,
    xg,
    mg,
    w,
    eg,
    eu,
    ed,
    rows,
    rhs,
    mid,
    rw,
    lhs,
    csend,
    crecv,
    keep,
    ysend,
    yrecv,
    zsend,
    zrecv,
    load_sem,
    x_send,
    x_recv,
    m_send,
    m_recv,
    w_send,
    w_recv,
    c_send,
    c_recv,
    y_send,
    y_recv,
    z_send,
    z_recv,
    h_send,
    h_recv,
):
    length = n // 4
    me = lax.axis_index("expert")
    z, y, c = me // 4, (me // 2) % 2, me % 2
    tokens, width = x_ref.shape
    per_block = rows.shape[0] // n
    part = w.shape[1] // n
    ff = eg.shape[1]
    bf16 = jnp.bfloat16

    def block(which):
        return pl.ds(pl.multiple_of(which * tokens, tokens), tokens)

    def place(zz, yy, cc):
        return zz * 4 + yy * 2 + cc

    right, left = place(z + 1, y, c), place(z - 1, y, c)
    across, sibling = place(z, 1 - y, c), place(z, y, 1 - c)

    loads = [
        pltpu.make_async_copy(src, dst, load_sem.at[i])
        for i, (src, dst) in enumerate(((eg_hbm, eg), (eu_hbm, eu), (ed_hbm, ed)))
    ]
    for load in loads:
        load.start()

    barrier = pltpu.get_barrier_semaphore()
    for step in range(1, n):
        pl.semaphore_signal(
            barrier, inc=1, device_id={"expert": lax.rem(me + step, n)}, device_id_type=MESH
        )
    group_at = lax.axis_index("groups")
    for other in range(1, spread):
        pl.semaphore_signal(
            barrier,
            inc=1,
            device_id={"groups": lax.rem(group_at + other, spread)},
            device_id_type=MESH,
        )
    xg[block(me), :] = x_ref[...]
    mg[me] = meta_ref[...]
    pl.semaphore_wait(barrier, n - 1 + spread - 1)

    def remote(src, dst, send, recv, target):
        return pltpu.make_async_remote_copy(
            src_ref=src,
            dst_ref=dst,
            send_sem=send,
            recv_sem=recv,
            device_id={"expert": target},
            device_id_type=MESH,
        )

    def block_copies(which, way, target):
        return (
            remote(xg.at[block(which)], xg.at[block(which)], x_send.at[way, which], x_recv.at[which], target),
            remote(mg.at[which], mg.at[which], m_send.at[way, which], m_recv.at[which], target),
        )

    def send_block(which, way, target):
        for copy in block_copies(which, way, target):
            copy.start()

    def sent_block(which, way, target):
        for copy in block_copies(which, way, target):
            copy.wait_send()

    def got_block(which):
        for copy in block_copies(which, 0, sibling):
            copy.wait_recv()

    share = w.shape[0] // spread
    own_share = pl.ds(pl.multiple_of(lax.rem(group_at, spread) * share, share), share)

    def weight_columns(source):
        return pl.ds(pl.multiple_of(source * part, part), part)

    def weight_copy(step):
        target = lax.rem(me + step, n)
        return remote(
            wsend_ref.at[target, own_share],
            w.at[own_share, weight_columns(me)],
            w_send.at[step],
            w_recv.at[me],
            target,
        )

    def weight_landing(step):
        source = lax.rem(me + step, n)
        return remote(
            wsend_ref.at[source, own_share],
            w.at[own_share, weight_columns(source)],
            w_send.at[step],
            w_recv.at[source],
            source,
        )

    def hand_on(step):
        return pltpu.make_async_remote_copy(
            src_ref=w.at[own_share],
            dst_ref=w.at[own_share],
            send_sem=h_send.at[step],
            recv_sem=h_recv.at[step],
            device_id={"groups": lax.rem(group_at + step, spread)},
            device_id_type=MESH,
        )

    chunk = 4 * per_block

    def landed_share(step):
        source = lax.rem(group_at + spread - step, spread)
        landed = pl.ds(pl.multiple_of(source * share, share), share)
        return pltpu.make_async_remote_copy(
            src_ref=w.at[landed],
            dst_ref=w.at[landed],
            send_sem=h_send.at[step],
            recv_sem=h_recv.at[step],
            device_id={"groups": lax.rem(group_at + step, spread)},
            device_id_type=MESH,
        )

    def route_rows(which, index):
        info = mg[which]
        spot = lax.broadcasted_iota(jnp.int32, (per_block, tokens), 0).astype(jnp.float32)
        base = (me * per_block).astype(jnp.float32)
        near = info - base
        first = spot == near[0:1, :]
        second = spot == near[1:2, :]
        pick = jnp.where(first | second, 1.0, 0.0).astype(bf16)
        scale = jnp.where(first, info[2:3, :], 0.0) + jnp.where(second, info[3:4, :], 0.0)
        spots = pl.ds(pl.multiple_of(which * per_block, per_block), per_block)
        rows[spots, :] = jnp.dot(
            pick, xg[block(which), :], preferred_element_type=jnp.float32
        ).astype(bf16)
        rw[spots, :] = jnp.broadcast_to(jnp.sum(scale, axis=1, keepdims=True), (per_block, 128))
        held = (near >= 0) & (near < per_block)
        wide = jnp.where(held, near + (index * per_block).astype(jnp.float32), -1.0)
        spread_spot = lax.broadcasted_iota(jnp.int32, (chunk, tokens), 0).astype(jnp.float32)
        wide_pick = jnp.where(
            (spread_spot == wide[0:1, :]) | (spread_spot == wide[1:2, :]), 1.0, 0.0
        )
        lhs[block(which), 0:chunk] = wide_pick.T.astype(bf16)

    tile = ff // 3 if ff % 384 == 0 else ff

    def expert_group(zz):
        def one_block(index, carry):
            route_rows(zz * 4 + index, index)
            return carry

        lax.fori_loop(0, 4, one_block, 0)
        spots = pl.ds(pl.multiple_of(zz * chunk, chunk), chunk)

        def hidden_tile(at, inner):
            columns = pl.ds(pl.multiple_of(at * tile, 128), tile)
            taken = rows[spots, :]
            gate = jnp.dot(taken, eg[:, columns], preferred_element_type=jnp.float32)
            up = jnp.dot(taken, eu[:, columns], preferred_element_type=jnp.float32)
            mid[:, columns] = (gate * jax.nn.sigmoid(gate) * up).astype(bf16)
            return inner

        lax.fori_loop(0, ff // tile, hidden_tile, 0)

        def out_tile(at, inner):
            columns = pl.ds(pl.multiple_of(at * 512, 512), 512)
            result = jnp.dot(mid[...], ed[:, columns], preferred_element_type=jnp.float32)
            rhs[zz, 0:chunk, columns] = (result * rw[spots, 0:1]).astype(bf16)
            return inner

        lax.fori_loop(0, width // 512, out_tile, 0)

    def shared_group(zz):
        spots = pl.ds(pl.multiple_of(zz * 4 * tokens, tokens), 4 * tokens)
        both = lax.dot_general(
            xg[spots, :], w[0 : 2 * fp, :], (((1,), (1,)), ((), ())), preferred_element_type=jnp.float32
        )
        gate, up = both[:, :fp], both[:, fp:]
        lhs[spots, chunk : chunk + fp] = (gate * jax.nn.sigmoid(gate) * up).astype(bf16)
        rhs[zz, chunk : chunk + fp, :] = w[2 * fp : 3 * fp, :]

    def partial_sum(zz, yy, cc):
        return jnp.dot(
            lhs[block(place(zz, yy, cc)), 0 : chunk + fp],
            rhs[zz],
            preferred_element_type=jnp.float32,
        )

    def core_copy(zz, yy):
        at = yy * length + zz
        return remote(csend.at[at], crecv.at[at], c_send.at[at], c_recv.at[at], sibling)

    def y_copy(zz):
        return remote(ysend.at[zz], yrecv.at[zz], y_send.at[zz], y_recv.at[zz], across)

    def z_copy(way, zz, target):
        return remote(zsend.at[zz], zrecv.at[way, zz], z_send.at[zz], z_recv.at[way, zz], target)

    def y_step(step):
        zs = stage_order(step, z, length)
        for yy in (1 - y, y):
            csend[yy * length + zs] = partial_sum(zs, yy, 1 - c).astype(bf16)
            core_copy(zs, yy).start()
        keep[zs] = partial_sum(zs, 1 - y, c)
        core_copy(zs, 1 - y).wait_recv()
        ysend[zs] = (keep[zs] + crecv[(1 - y) * length + zs].astype(jnp.float32)).astype(bf16)
        y_copy(zs).start()
        keep[zs] = partial_sum(zs, y, c)
        core_copy(zs, y).wait_recv()
        keep[zs] += crecv[y * length + zs].astype(jnp.float32)

    def z_step(step):
        zp = stage_order(step, z, length)
        y_copy(zp).wait_recv()
        keep[zp] += yrecv[zp].astype(jnp.float32)

        @pl.when((zp >= z) & (z > 0))
        def _():
            z_copy(0, zp, left).wait_recv()
            keep[zp] += zrecv[0, zp].astype(jnp.float32)

        @pl.when((zp <= z) & (z < length - 1))
        def _():
            z_copy(1, zp, right).wait_recv()
            keep[zp] += zrecv[1, zp].astype(jnp.float32)

        if step < length - 1:
            zsend[zp] = keep[zp].astype(bf16)

            @pl.when(zp > z)
            def _():
                z_copy(0, zp, right).start()

            @pl.when(zp < z)
            def _():
                z_copy(1, zp, left).start()

    def arrival(step):
        return stage_order(length - 1 - step, z, length)

    early = length - 2
    for step in range(length + 1):
        if step < length:
            zs = arrival(step)
            which = place(zs, y, c)
            if step > 0:
                got_block(which)

            @pl.when((zs <= z) & (z < length - 1))
            def _():
                send_block(which, 0, right)

            @pl.when((zs >= z) & (z > 0))
            def _():
                send_block(which, 1, left)

            send_block(which, 2, across)
            send_block(which, 3, sibling)
        if step == 0:
            for other in range(1, n):
                weight_copy(other).start()
            w[own_share, weight_columns(me)] = wsend_ref[me, own_share]
            for load in loads:
                load.wait()
            continue
        if step == 2:
            for other in range(1, n):
                weight_landing(other).wait_recv()
            for other in range(1, spread):
                hand_on(other).start()
        if step == length - 1:
            for other in range(1, spread):
                landed_share(other).wait_recv()
            for done in range(length - 2):
                shared_group(arrival(done))
        zp = arrival(step - 1)
        far = place(zp, 1 - y, c)
        got_block(far)
        send_block(far, 3, sibling)
        got_block(place(zp, y, 1 - c))
        got_block(place(zp, 1 - y, 1 - c))
        expert_group(zp)
        if step >= length - 1:
            shared_group(zp)
        if step == length - 1:
            y_step(early)

    later = [step for step in range(length) if step != early]
    y_step(later[0])
    sent = 0
    for step in later[1:]:
        y_step(step)
        z_step(sent)
        sent += 1
    for step in range(sent, length):
        z_step(step)

    out_ref[...] = keep[z]

    for step in range(length):
        zs = stage_order(step, z, length)
        which = place(zs, y, c)

        @pl.when((zs <= z) & (z < length - 1))
        def _():
            sent_block(which, 0, right)

        @pl.when((zs >= z) & (z > 0))
        def _():
            sent_block(which, 1, left)

        sent_block(which, 2, across)
        sent_block(which, 3, sibling)
        sent_block(place(zs, 1 - y, c), 3, sibling)
        core_copy(zs, 1 - y).wait_send()
        core_copy(zs, y).wait_send()
        y_copy(zs).wait_send()
        if step < length - 1:

            @pl.when(zs > z)
            def _():
                z_copy(0, zs, right).wait_send()

            @pl.when(zs < z)
            def _():
                z_copy(1, zs, left).wait_send()

    for other in range(1, n):
        weight_copy(other).wait_send()
    for other in range(1, spread):
        hand_on(other).wait_send()


def exchange(n, spread, fp, slots, flat_rows, meta, wsend, w_gate, w_up, w_down):
    length = n // 4
    tokens, width = flat_rows.shape
    ff = w_gate.shape[1]
    bf16, f32 = jnp.bfloat16, jnp.float32
    whole = pl.BlockSpec(memory_space=pltpu.VMEM)
    away = pl.BlockSpec(memory_space=pl.ANY)
    sems = pltpu.SemaphoreType.DMA
    return pl.pallas_call(
        functools.partial(exchange_kernel, n, spread, fp),
        out_shape=jax.ShapeDtypeStruct((tokens, width), f32),
        in_specs=[whole, whole, whole, away, away, away],
        out_specs=whole,
        scratch_shapes=[
            pltpu.VMEM((n * tokens, width), bf16),
            pltpu.VMEM((n,) + meta.shape, f32),
            pltpu.VMEM((3 * fp, width), bf16),
            pltpu.VMEM((width, ff), bf16),
            pltpu.VMEM((width, ff), bf16),
            pltpu.VMEM((ff, width), bf16),
            pltpu.VMEM((n * slots, width), bf16),
            pltpu.VMEM((length, 4 * slots + fp, width), bf16),
            pltpu.VMEM((4 * slots, ff), bf16),
            pltpu.VMEM((n * slots, 128), f32),
            pltpu.VMEM((n * tokens, -(-(4 * slots + fp) // 128) * 128), bf16),
            pltpu.VMEM((2 * length, tokens, width), bf16),
            pltpu.VMEM((2 * length, tokens, width), bf16),
            pltpu.VMEM((length, tokens, width), f32),
            pltpu.VMEM((length, tokens, width), bf16),
            pltpu.VMEM((length, tokens, width), bf16),
            pltpu.VMEM((length, tokens, width), bf16),
            pltpu.VMEM((2, length, tokens, width), bf16),
            sems((3,)),
            sems((4, n)),
            sems((n,)),
            sems((4, n)),
            sems((n,)),
            sems((n,)),
            sems((n,)),
            sems((2 * length,)),
            sems((2 * length,)),
            sems((length,)),
            sems((length,)),
            sems((length,)),
            sems((2, length)),
            sems((spread,)),
            sems((spread,)),
        ],
        compiler_params=pltpu.CompilerParams(
            collective_id=0, has_side_effects=True, vmem_limit_bytes=60 * 1024 * 1024
        ),
    )(flat_rows, meta, wsend, w_gate, w_up, w_down)


def fits(n, tokens, width, slots, ff, local_count, experts):
    moved = n * tokens * width * 2 * 4
    weights = 3 * width * ff * 2 + 2 * n * slots * width * 2
    return (
        n % 4 == 0
        and n > 8
        and experts == n
        and local_count == 1
        and tokens == 128
        and width % (n * 128) == 0
        and width % 512 == 0
        and ff % 128 == 0
        and slots % 32 == 0
        and moved + weights < 56 * 1024 * 1024
    )


def local(
    n,
    parts,
    tokens,
    route_ids,
    route_slots,
    mod_shift,
    mod_scale,
    mod_gate,
    guidance,
    router_weight,
    expert_gate,
    expert_up,
    expert_down,
    shared_gate,
    shared_up,
    shared_down,
    head_weight,
):
    model_width = tokens.shape[-1]
    per_half = tokens.shape[1]
    choices_each = route_ids.shape[2]
    experts = router_weight.shape[1]
    capacity = 2 * choices_each * per_half // experts
    inputs = tokens.astype(jnp.float32)
    modulated = (layer_norm(inputs) * (1.0 + mod_scale[:, None, :]) + mod_shift[:, None, :]).astype(
        jnp.bfloat16
    )
    flat_rows = modulated.reshape(2 * per_half, model_width)
    logits = jnp.dot(flat_rows, router_weight, preferred_element_type=jnp.float32).reshape(
        2, per_half, experts
    )
    chosen_expert = route_ids[..., None] == jnp.arange(experts, dtype=jnp.int32)
    picked = jnp.sum(jnp.where(chosen_expert, logits[:, :, None, :], 0.0), axis=3)
    affinity = jax.nn.sigmoid(picked)
    weights = affinity / jnp.sum(affinity, axis=2, keepdims=True)
    half_index = jnp.arange(2, dtype=jnp.int32)
    slot_place = (route_ids * 2 + half_index[:, None, None]) * capacity + route_slots
    slots = 2 * capacity
    if choices_each == 2 and fits(
        n,
        2 * per_half,
        model_width,
        slots,
        expert_gate.shape[2],
        expert_gate.shape[0],
        experts,
    ):
        share = shared_gate.shape[1] // n
        fp = tile_rows(share)
        spread = parts if 3 * fp % (16 * parts) == 0 else 1
        pieces = [
            jnp.pad(piece.reshape(n, share, -1), ((0, 0), (0, fp - share), (0, 0)))
            for piece in (shared_gate.T, shared_up.T, shared_down)
        ]
        wsend = jnp.concatenate(pieces, axis=1)
        flat_place = slot_place.reshape(2 * per_half, choices_each).astype(jnp.float32)
        flat_weight = weights.reshape(2 * per_half, choices_each)
        meta = jnp.concatenate([flat_place, flat_weight], axis=1).T
        meta = jnp.pad(meta, ((0, 8 - meta.shape[0]), (0, 0)))
        added = exchange(
            n, spread, fp, slots, flat_rows, meta, wsend, expert_gate[0], expert_up[0], expert_down[0]
        ).reshape(2, per_half, model_width)
    else:
        full_gate, full_up, full_down = (
            lax.all_gather(shared_gate, "expert", axis=0, tiled=True),
            lax.all_gather(shared_up, "expert", axis=0, tiled=True),
            lax.all_gather(shared_down, "expert", axis=1, tiled=True),
        )
        gate_sum = jnp.dot(flat_rows, full_gate, preferred_element_type=jnp.float32)
        up_sum = jnp.dot(flat_rows, full_up, preferred_element_type=jnp.float32)
        shared_hidden = (jax.nn.silu(gate_sum) * up_sum).astype(jnp.bfloat16)
        shared = jnp.dot(shared_hidden, full_down, preferred_element_type=jnp.float32)
        shared = shared.reshape(2, per_half, model_width)
        matrix = dispatch_matrix(slot_place.reshape(2 * per_half, choices_each), 2 * experts * capacity)
        outgoing = jnp.dot(matrix, flat_rows, preferred_element_type=jnp.float32).astype(jnp.bfloat16)
        outgoing = outgoing.reshape(experts, 2, capacity, model_width)
        answered = expert_block(
            lax.all_to_all(outgoing, "expert", split_axis=0, concat_axis=0, tiled=True),
            expert_gate,
            expert_up,
            expert_down,
        )
        returned = lax.all_to_all(answered, "expert", split_axis=0, concat_axis=0, tiled=True)
        chosen = jnp.take(returned.reshape(-1, model_width), slot_place.reshape(-1), axis=0)
        chosen = chosen.reshape(2, per_half, choices_each, model_width)
        routed = jnp.sum(weights[..., None] * chosen.astype(jnp.float32), axis=2)
        added = routed + shared
    hidden_out = (inputs + mod_gate[:, None, :] * added).astype(jnp.bfloat16)
    final_norm = layer_norm(hidden_out.astype(jnp.float32)).astype(jnp.bfloat16)
    predicted = jnp.dot(
        final_norm.reshape(2 * per_half, model_width),
        head_weight,
        preferred_element_type=jnp.float32,
    )
    predicted = predicted.reshape(2, per_half, head_weight.shape[1])
    guided = predicted[1] + guidance[0] * (predicted[0] - predicted[1])
    return (hidden_out, guided)


def solution(mesh):
    in_specs = (
        P(None, ("groups", "expert"), None),
        P(None, ("groups", "expert"), None),
        P(None, ("groups", "expert"), None),
        P("groups", None),
        P("groups", None),
        P("groups", None),
        P("groups"),
        P(),
        P("expert", None, None),
        P("expert", None, None),
        P("expert", None, None),
        P("expert", None),
        P("expert", None),
        P(None, "expert"),
        P(),
    )
    out_specs = (P(None, ("groups", "expert"), None), P(("groups", "expert"), None))
    run = functools.partial(local, mesh.shape["expert"], mesh.shape["groups"])
    return jax.shard_map(run, mesh=mesh, in_specs=in_specs, out_specs=out_specs, check_vma=False)
```

```python
import functools
import math

import jax
import jax.numpy as jnp
from jax import lax
from jax.experimental import pallas as pl
from jax.experimental.pallas import tpu as pltpu
from jax.sharding import PartitionSpec as P

epsilon = 1e-06
MESH = pl.DeviceIdType.MESH


def layer_norm(values):
    center = values - jnp.mean(values, axis=-1, keepdims=True)
    spread = jnp.mean(center * center, axis=-1, keepdims=True)
    return center * lax.rsqrt(spread + epsilon)


def expert_block(received, w_gate, w_up, w_down):
    array_shape = received.shape
    local_count = w_gate.shape[0]
    middle = math.prod(array_shape[1:-1])
    row_block = received.reshape(
        array_shape[0] // local_count, local_count, middle, array_shape[-1]
    )
    gate_part = jnp.einsum("semd,edf->semf", row_block, w_gate, preferred_element_type=jnp.float32)
    up_part = jnp.einsum("semd,edf->semf", row_block, w_up, preferred_element_type=jnp.float32)
    hidden = (jax.nn.silu(gate_part) * up_part).astype(jnp.bfloat16)
    result = jnp.einsum("semf,efd->semd", hidden, w_down, preferred_element_type=jnp.float32)
    return result.astype(jnp.bfloat16).reshape(array_shape)


def dispatch_matrix(slot_place, slot_total):
    slot_index = jnp.arange(slot_total, dtype=jnp.int32)
    matches = slot_index[:, None, None] == slot_place[None, :, :]
    return jnp.sum(matches.astype(jnp.int32), axis=2).astype(jnp.bfloat16)


def tile_rows(count):
    return -(-count // 16) * 16


def stage_order(step, place, length):
    if step == length - 1:
        return place
    down = length - 1 - step
    down = down - jnp.where(down <= place, 1, 0)
    up = step + jnp.where(place <= step, 1, 0)
    return jnp.where(place < length // 2, down, up)


def exchange_kernel(
    n,
    spread,
    fp,
    x_ref,
    meta_ref,
    shift_ref,
    scale_ref,
    router_ref,
    wsend_ref,
    eg_hbm,
    eu_hbm,
    ed_hbm,
    out_ref,
    xg,
    mg,
    w,
    eg,
    eu,
    ed,
    rows,
    rhs,
    mid,
    rw,
    lhs,
    csend,
    crecv,
    keep,
    ysend,
    yrecv,
    zsend,
    zrecv,
    load_sem,
    x_send,
    x_recv,
    m_send,
    m_recv,
    w_send,
    w_recv,
    c_send,
    c_recv,
    y_send,
    y_recv,
    z_send,
    z_recv,
    h_send,
    h_recv,
):
    length = n // 4
    me = lax.axis_index("expert")
    z, y, c = me // 4, (me // 2) % 2, me % 2
    tokens, width = x_ref.shape
    per_block = rows.shape[0] // n
    part = w.shape[1] // n
    ff = eg.shape[1]
    bf16 = jnp.bfloat16

    def block(which):
        return pl.ds(pl.multiple_of(which * tokens, tokens), tokens)

    def place(zz, yy, cc):
        return zz * 4 + yy * 2 + cc

    right, left = place(z + 1, y, c), place(z - 1, y, c)
    across, sibling = place(z, 1 - y, c), place(z, y, 1 - c)

    loads = [
        pltpu.make_async_copy(src, dst, load_sem.at[i])
        for i, (src, dst) in enumerate(((eg_hbm, eg), (eu_hbm, eu), (ed_hbm, ed)))
    ]
    for load in loads:
        load.start()

    barrier = pltpu.get_barrier_semaphore()
    for step in range(1, n):
        pl.semaphore_signal(
            barrier, inc=1, device_id={"expert": lax.rem(me + step, n)}, device_id_type=MESH
        )
    group_at = lax.axis_index("groups")
    for other in range(1, spread):
        pl.semaphore_signal(
            barrier,
            inc=1,
            device_id={"groups": lax.rem(group_at + other, spread)},
            device_id_type=MESH,
        )
    per_half = tokens // 2
    for half in range(2):
        values = x_ref[half * per_half : (half + 1) * per_half, :].astype(jnp.float32)
        normed = layer_norm(values)
        modulated = normed * (1.0 + scale_ref[half : half + 1, :]) + shift_ref[half : half + 1, :]
        spot = pl.multiple_of(me * tokens + half * per_half, per_half)
        xg[pl.ds(spot, per_half), :] = modulated.astype(bf16)
    logits = lax.dot_general(
        router_ref[...],
        xg[block(me), :],
        (((1,), (1,)), ((), ())),
        preferred_element_type=jnp.float32,
    )
    chosen = meta_ref[...]
    expert_row = lax.broadcasted_iota(jnp.int32, logits.shape, 0).astype(jnp.float32)
    affinity = [
        jax.nn.sigmoid(
            jnp.sum(jnp.where(expert_row == chosen[k : k + 1, :], logits, 0.0), axis=0, keepdims=True)
        )
        for k in (2, 3)
    ]
    total = affinity[0] + affinity[1]
    row_at = lax.broadcasted_iota(jnp.int32, chosen.shape, 0)
    mg[me] = jnp.where(
        row_at == 2, affinity[0] / total, jnp.where(row_at == 3, affinity[1] / total, chosen)
    )
    pl.semaphore_wait(barrier, n - 1 + spread - 1)

    def remote(src, dst, send, recv, target):
        return pltpu.make_async_remote_copy(
            src_ref=src,
            dst_ref=dst,
            send_sem=send,
            recv_sem=recv,
            device_id={"expert": target},
            device_id_type=MESH,
        )

    def block_copies(which, way, target):
        return (
            remote(xg.at[block(which)], xg.at[block(which)], x_send.at[way, which], x_recv.at[which], target),
            remote(mg.at[which], mg.at[which], m_send.at[way, which], m_recv.at[which], target),
        )

    def send_block(which, way, target):
        for copy in block_copies(which, way, target):
            copy.start()

    def sent_block(which, way, target):
        for copy in block_copies(which, way, target):
            copy.wait_send()

    def got_block(which):
        for copy in block_copies(which, 0, sibling):
            copy.wait_recv()

    share = w.shape[0] // spread
    own_share = pl.ds(pl.multiple_of(lax.rem(group_at, spread) * share, share), share)

    def weight_columns(source):
        return pl.ds(pl.multiple_of(source * part, part), part)

    def weight_copy(step):
        target = lax.rem(me + step, n)
        return remote(
            wsend_ref.at[target, own_share],
            w.at[own_share, weight_columns(me)],
            w_send.at[step],
            w_recv.at[me],
            target,
        )

    def weight_landing(step):
        source = lax.rem(me + step, n)
        return remote(
            wsend_ref.at[source, own_share],
            w.at[own_share, weight_columns(source)],
            w_send.at[step],
            w_recv.at[source],
            source,
        )

    def hand_on(step):
        return pltpu.make_async_remote_copy(
            src_ref=w.at[own_share],
            dst_ref=w.at[own_share],
            send_sem=h_send.at[step],
            recv_sem=h_recv.at[step],
            device_id={"groups": lax.rem(group_at + step, spread)},
            device_id_type=MESH,
        )

    chunk = 4 * per_block

    def landed_share(step):
        source = lax.rem(group_at + spread - step, spread)
        landed = pl.ds(pl.multiple_of(source * share, share), share)
        return pltpu.make_async_remote_copy(
            src_ref=w.at[landed],
            dst_ref=w.at[landed],
            send_sem=h_send.at[step],
            recv_sem=h_recv.at[step],
            device_id={"groups": lax.rem(group_at + step, spread)},
            device_id_type=MESH,
        )

    def route_rows(which, index):
        info = mg[which]
        spot = lax.broadcasted_iota(jnp.int32, (per_block, tokens), 0).astype(jnp.float32)
        base = (me * per_block).astype(jnp.float32)
        near = info - base
        first = spot == near[0:1, :]
        second = spot == near[1:2, :]
        pick = jnp.where(first | second, 1.0, 0.0).astype(bf16)
        scale = jnp.where(first, info[2:3, :], 0.0) + jnp.where(second, info[3:4, :], 0.0)
        spots = pl.ds(pl.multiple_of(which * per_block, per_block), per_block)
        rows[spots, :] = jnp.dot(
            pick, xg[block(which), :], preferred_element_type=jnp.float32
        ).astype(bf16)
        rw[spots, :] = jnp.broadcast_to(jnp.sum(scale, axis=1, keepdims=True), (per_block, 128))
        held = (near >= 0) & (near < per_block)
        wide = jnp.where(held, near + (index * per_block).astype(jnp.float32), -1.0)
        spread_spot = lax.broadcasted_iota(jnp.int32, (chunk, tokens), 0).astype(jnp.float32)
        wide_pick = jnp.where(
            (spread_spot == wide[0:1, :]) | (spread_spot == wide[1:2, :]), 1.0, 0.0
        )
        lhs[block(which), 0:chunk] = wide_pick.T.astype(bf16)

    tile = ff // 3 if ff % 384 == 0 else ff

    def expert_group(zz):
        def one_block(index, carry):
            route_rows(zz * 4 + index, index)
            return carry

        lax.fori_loop(0, 4, one_block, 0)
        spots = pl.ds(pl.multiple_of(zz * chunk, chunk), chunk)

        def hidden_tile(at, inner):
            columns = pl.ds(pl.multiple_of(at * tile, 128), tile)
            taken = rows[spots, :]
            gate = jnp.dot(taken, eg[:, columns], preferred_element_type=jnp.float32)
            up = jnp.dot(taken, eu[:, columns], preferred_element_type=jnp.float32)
            mid[:, columns] = (gate * jax.nn.sigmoid(gate) * up).astype(bf16)
            return inner

        lax.fori_loop(0, ff // tile, hidden_tile, 0)

        def out_tile(at, inner):
            columns = pl.ds(pl.multiple_of(at * 512, 512), 512)
            result = jnp.dot(mid[...], ed[:, columns], preferred_element_type=jnp.float32)
            rhs[zz, 0:chunk, columns] = (result * rw[spots, 0:1]).astype(bf16)
            return inner

        lax.fori_loop(0, width // 512, out_tile, 0)

    def shared_group(zz):
        spots = pl.ds(pl.multiple_of(zz * 4 * tokens, tokens), 4 * tokens)
        both = lax.dot_general(
            xg[spots, :], w[0 : 2 * fp, :], (((1,), (1,)), ((), ())), preferred_element_type=jnp.float32
        )
        gate, up = both[:, :fp], both[:, fp:]
        lhs[spots, chunk : chunk + fp] = (gate * jax.nn.sigmoid(gate) * up).astype(bf16)
        rhs[zz, chunk : chunk + fp, :] = w[2 * fp : 3 * fp, :]

    def partial_sum(zz, yy, cc):
        return jnp.dot(
            lhs[block(place(zz, yy, cc)), 0 : chunk + fp],
            rhs[zz],
            preferred_element_type=jnp.float32,
        )

    def core_copy(zz, yy):
        at = yy * length + zz
        return remote(csend.at[at], crecv.at[at], c_send.at[at], c_recv.at[at], sibling)

    def y_copy(zz):
        return remote(ysend.at[zz], yrecv.at[zz], y_send.at[zz], y_recv.at[zz], across)

    def z_copy(way, zz, target):
        return remote(zsend.at[zz], zrecv.at[way, zz], z_send.at[zz], z_recv.at[way, zz], target)

    def y_step(step):
        zs = stage_order(step, z, length)
        for yy in (1 - y, y):
            csend[yy * length + zs] = partial_sum(zs, yy, 1 - c).astype(bf16)
            core_copy(zs, yy).start()
        keep[zs] = partial_sum(zs, 1 - y, c)
        core_copy(zs, 1 - y).wait_recv()
        ysend[zs] = (keep[zs] + crecv[(1 - y) * length + zs].astype(jnp.float32)).astype(bf16)
        y_copy(zs).start()
        keep[zs] = partial_sum(zs, y, c)
        core_copy(zs, y).wait_recv()
        keep[zs] += crecv[y * length + zs].astype(jnp.float32)

    def z_step(step):
        zp = stage_order(step, z, length)
        y_copy(zp).wait_recv()
        keep[zp] += yrecv[zp].astype(jnp.float32)

        @pl.when((zp >= z) & (z > 0))
        def _():
            z_copy(0, zp, left).wait_recv()
            keep[zp] += zrecv[0, zp].astype(jnp.float32)

        @pl.when((zp <= z) & (z < length - 1))
        def _():
            z_copy(1, zp, right).wait_recv()
            keep[zp] += zrecv[1, zp].astype(jnp.float32)

        if step < length - 1:
            zsend[zp] = keep[zp].astype(bf16)

            @pl.when(zp > z)
            def _():
                z_copy(0, zp, right).start()

            @pl.when(zp < z)
            def _():
                z_copy(1, zp, left).start()

    def arrival(step):
        return stage_order(length - 1 - step, z, length)

    early = length - 2
    for step in range(length + 1):
        if step < length:
            zs = arrival(step)
            which = place(zs, y, c)
            if step > 0:
                got_block(which)

            @pl.when((zs <= z) & (z < length - 1))
            def _():
                send_block(which, 0, right)

            @pl.when((zs >= z) & (z > 0))
            def _():
                send_block(which, 1, left)

            send_block(which, 2, across)
            send_block(which, 3, sibling)
        if step == 0:
            for other in range(1, n):
                weight_copy(other).start()
            w[own_share, weight_columns(me)] = wsend_ref[me, own_share]
            for load in loads:
                load.wait()
            continue
        if step == 2:
            for other in range(1, n):
                weight_landing(other).wait_recv()
            for other in range(1, spread):
                hand_on(other).start()
        if step == length - 1:
            for other in range(1, spread):
                landed_share(other).wait_recv()
            for done in range(length - 2):
                shared_group(arrival(done))
        zp = arrival(step - 1)
        far = place(zp, 1 - y, c)
        got_block(far)
        send_block(far, 3, sibling)
        got_block(place(zp, y, 1 - c))
        got_block(place(zp, 1 - y, 1 - c))
        expert_group(zp)
        if step >= length - 1:
            shared_group(zp)
        if step == length - 1:
            y_step(early)

    later = [step for step in range(length) if step != early]
    y_step(later[0])
    sent = 0
    for step in later[1:]:
        y_step(step)
        z_step(sent)
        sent += 1
    for step in range(sent, length):
        z_step(step)

    out_ref[...] = keep[z]

    for step in range(length):
        zs = stage_order(step, z, length)
        which = place(zs, y, c)

        @pl.when((zs <= z) & (z < length - 1))
        def _():
            sent_block(which, 0, right)

        @pl.when((zs >= z) & (z > 0))
        def _():
            sent_block(which, 1, left)

        sent_block(which, 2, across)
        sent_block(which, 3, sibling)
        sent_block(place(zs, 1 - y, c), 3, sibling)
        core_copy(zs, 1 - y).wait_send()
        core_copy(zs, y).wait_send()
        y_copy(zs).wait_send()
        if step < length - 1:

            @pl.when(zs > z)
            def _():
                z_copy(0, zs, right).wait_send()

            @pl.when(zs < z)
            def _():
                z_copy(1, zs, left).wait_send()

    for other in range(1, n):
        weight_copy(other).wait_send()
    for other in range(1, spread):
        hand_on(other).wait_send()


def exchange(n, spread, fp, slots, flat_rows, meta, shift, scale, router, wsend, w_gate, w_up, w_down):
    length = n // 4
    tokens, width = flat_rows.shape
    ff = w_gate.shape[1]
    bf16, f32 = jnp.bfloat16, jnp.float32
    whole = pl.BlockSpec(memory_space=pltpu.VMEM)
    away = pl.BlockSpec(memory_space=pl.ANY)
    sems = pltpu.SemaphoreType.DMA
    return pl.pallas_call(
        functools.partial(exchange_kernel, n, spread, fp),
        out_shape=jax.ShapeDtypeStruct((tokens, width), f32),
        in_specs=[whole] * 6 + [away] * 3,
        out_specs=whole,
        scratch_shapes=[
            pltpu.VMEM((n * tokens, width), bf16),
            pltpu.VMEM((n,) + meta.shape, f32),
            pltpu.VMEM((3 * fp, width), bf16),
            pltpu.VMEM((width, ff), bf16),
            pltpu.VMEM((width, ff), bf16),
            pltpu.VMEM((ff, width), bf16),
            pltpu.VMEM((n * slots, width), bf16),
            pltpu.VMEM((length, 4 * slots + fp, width), bf16),
            pltpu.VMEM((4 * slots, ff), bf16),
            pltpu.VMEM((n * slots, 128), f32),
            pltpu.VMEM((n * tokens, -(-(4 * slots + fp) // 128) * 128), bf16),
            pltpu.VMEM((2 * length, tokens, width), bf16),
            pltpu.VMEM((2 * length, tokens, width), bf16),
            pltpu.VMEM((length, tokens, width), f32),
            pltpu.VMEM((length, tokens, width), bf16),
            pltpu.VMEM((length, tokens, width), bf16),
            pltpu.VMEM((length, tokens, width), bf16),
            pltpu.VMEM((2, length, tokens, width), bf16),
            sems((3,)),
            sems((4, n)),
            sems((n,)),
            sems((4, n)),
            sems((n,)),
            sems((n,)),
            sems((n,)),
            sems((2 * length,)),
            sems((2 * length,)),
            sems((length,)),
            sems((length,)),
            sems((length,)),
            sems((2, length)),
            sems((spread,)),
            sems((spread,)),
        ],
        compiler_params=pltpu.CompilerParams(
            collective_id=0, has_side_effects=True, vmem_limit_bytes=60 * 1024 * 1024
        ),
    )(flat_rows, meta, shift, scale, router, wsend, w_gate, w_up, w_down)


def fits(n, tokens, width, slots, ff, local_count, experts):
    moved = n * tokens * width * 2 * 4
    weights = 3 * width * ff * 2 + 2 * n * slots * width * 2
    return (
        n % 4 == 0
        and n > 8
        and experts == n
        and local_count == 1
        and tokens == 128
        and width % (n * 128) == 0
        and width % 512 == 0
        and ff % 128 == 0
        and slots % 32 == 0
        and moved + weights < 56 * 1024 * 1024
    )


def local(
    n,
    parts,
    tokens,
    route_ids,
    route_slots,
    mod_shift,
    mod_scale,
    mod_gate,
    guidance,
    router_weight,
    expert_gate,
    expert_up,
    expert_down,
    shared_gate,
    shared_up,
    shared_down,
    head_weight,
):
    model_width = tokens.shape[-1]
    per_half = tokens.shape[1]
    choices_each = route_ids.shape[2]
    experts = router_weight.shape[1]
    capacity = 2 * choices_each * per_half // experts
    inputs = tokens.astype(jnp.float32)
    half_index = jnp.arange(2, dtype=jnp.int32)
    slot_place = (route_ids * 2 + half_index[:, None, None]) * capacity + route_slots
    slots = 2 * capacity
    if choices_each == 2 and fits(
        n,
        2 * per_half,
        model_width,
        slots,
        expert_gate.shape[2],
        expert_gate.shape[0],
        experts,
    ):
        share = shared_gate.shape[1] // n
        fp = tile_rows(share)
        spread = parts if 3 * fp % (16 * parts) == 0 else 1
        pieces = [
            jnp.pad(piece.reshape(n, share, -1), ((0, 0), (0, fp - share), (0, 0)))
            for piece in (shared_gate.T, shared_up.T, shared_down)
        ]
        wsend = jnp.concatenate(pieces, axis=1)
        flat_place = slot_place.reshape(2 * per_half, choices_each).astype(jnp.float32)
        flat_ids = route_ids.reshape(2 * per_half, choices_each).astype(jnp.float32)
        meta = jnp.concatenate([flat_place, flat_ids], axis=1).T
        meta = jnp.pad(meta, ((0, 8 - meta.shape[0]), (0, 0)))
        added = exchange(
            n,
            spread,
            fp,
            slots,
            tokens.reshape(2 * per_half, model_width),
            meta,
            mod_shift,
            mod_scale,
            router_weight.T,
            wsend,
            expert_gate[0],
            expert_up[0],
            expert_down[0],
        ).reshape(2, per_half, model_width)
    else:
        modulated = (layer_norm(inputs) * (1.0 + mod_scale[:, None, :]) + mod_shift[:, None, :]).astype(
            jnp.bfloat16
        )
        flat_rows = modulated.reshape(2 * per_half, model_width)
        logits = jnp.dot(flat_rows, router_weight, preferred_element_type=jnp.float32).reshape(
            2, per_half, experts
        )
        chosen_expert = route_ids[..., None] == jnp.arange(experts, dtype=jnp.int32)
        picked = jnp.sum(jnp.where(chosen_expert, logits[:, :, None, :], 0.0), axis=3)
        affinity = jax.nn.sigmoid(picked)
        weights = affinity / jnp.sum(affinity, axis=2, keepdims=True)
        full_gate, full_up, full_down = (
            lax.all_gather(shared_gate, "expert", axis=0, tiled=True),
            lax.all_gather(shared_up, "expert", axis=0, tiled=True),
            lax.all_gather(shared_down, "expert", axis=1, tiled=True),
        )
        gate_sum = jnp.dot(flat_rows, full_gate, preferred_element_type=jnp.float32)
        up_sum = jnp.dot(flat_rows, full_up, preferred_element_type=jnp.float32)
        shared_hidden = (jax.nn.silu(gate_sum) * up_sum).astype(jnp.bfloat16)
        shared = jnp.dot(shared_hidden, full_down, preferred_element_type=jnp.float32)
        shared = shared.reshape(2, per_half, model_width)
        matrix = dispatch_matrix(slot_place.reshape(2 * per_half, choices_each), 2 * experts * capacity)
        outgoing = jnp.dot(matrix, flat_rows, preferred_element_type=jnp.float32).astype(jnp.bfloat16)
        outgoing = outgoing.reshape(experts, 2, capacity, model_width)
        answered = expert_block(
            lax.all_to_all(outgoing, "expert", split_axis=0, concat_axis=0, tiled=True),
            expert_gate,
            expert_up,
            expert_down,
        )
        returned = lax.all_to_all(answered, "expert", split_axis=0, concat_axis=0, tiled=True)
        chosen = jnp.take(returned.reshape(-1, model_width), slot_place.reshape(-1), axis=0)
        chosen = chosen.reshape(2, per_half, choices_each, model_width)
        routed = jnp.sum(weights[..., None] * chosen.astype(jnp.float32), axis=2)
        added = routed + shared
    hidden_out = (inputs + mod_gate[:, None, :] * added).astype(jnp.bfloat16)
    final_norm = layer_norm(hidden_out.astype(jnp.float32)).astype(jnp.bfloat16)
    predicted = jnp.dot(
        final_norm.reshape(2 * per_half, model_width),
        head_weight,
        preferred_element_type=jnp.float32,
    )
    predicted = predicted.reshape(2, per_half, head_weight.shape[1])
    guided = predicted[1] + guidance[0] * (predicted[0] - predicted[1])
    return (hidden_out, guided)


def solution(mesh):
    in_specs = (
        P(None, ("groups", "expert"), None),
        P(None, ("groups", "expert"), None),
        P(None, ("groups", "expert"), None),
        P("groups", None),
        P("groups", None),
        P("groups", None),
        P("groups"),
        P(),
        P("expert", None, None),
        P("expert", None, None),
        P("expert", None, None),
        P("expert", None),
        P("expert", None),
        P(None, "expert"),
        P(),
    )
    out_specs = (P(None, ("groups", "expert"), None), P(("groups", "expert"), None))
    run = functools.partial(local, mesh.shape["expert"], mesh.shape["groups"])
    return jax.shard_map(run, mesh=mesh, in_specs=in_specs, out_specs=out_specs, check_vma=False)
```
